32 devices in a mesh: slab: 2 (over y), tile: 4 (over z), gz: 2 (over x), ang: 2 (over core).
Axes of the slice: x: 2, y: 2, z: 4, core: 2. Of those that a mesh axis runs over, the one named last changes fastest.
Arguments:
- primal: float32 [32, 8192], P(('slab', 'gz'), 'tile'), parts along dimension 0, may hold values from -6 to 6
- dual: float32 [32, 64, 2048], P(('slab', 'gz'), ('ang', 'tile')), parts along dimension 0, may hold values from -6 to 6
- data: float32 [32, 64, 2048], P(('slab', 'gz'), ('ang', 'tile')), parts along dimension 0, may hold values from -6 to 6
- blocks: bfloat16 [4, 64, 2048, 128], P('tile', 'ang'), may hold values from -0.125 to 0.125
- offsets: int32 [4, 64], P(None, 'ang'), may hold values from 0 to 1920
- incidence: int32 [4, 64], P(None, 'ang'), may hold values 0 or 1
- dual_in: float32 [3, 32], replicated, may hold values from -4 to 4
- dual_bias: float32 [32], replicated, may hold values from -3 to 3
- dual_out: float32 [32], replicated, may hold values from -1 to 1
- kernel_in: float32 [3, 2, 32], replicated, may hold values from -2.5 to 2.5
- kernel_bias: float32 [32], replicated, may hold values from -3 to 3
- kernel_out: float32 [3, 32], replicated, may hold values from -0.625 to 0.625
- cot_primal: float32 [32, 8192], P(('slab', 'gz'), 'tile'), parts along dimension 0, may hold values from -6 to 6
- cot_dual: float32 [32, 64, 2048], P(('slab', 'gz'), ('ang', 'tile')), parts along dimension 0, may hold values from -6 to 6
Outputs:
- grad_primal: float32 [32, 8192], P(('slab', 'gz'), 'tile'), parts along dimension 0
- grad_dual: float32 [32, 64, 2048], P(('slab', 'gz'), ('ang', 'tile')), parts along dimension 0
- grad_data: float32 [32, 64, 2048], P(('slab', 'gz'), ('ang', 'tile')), parts along dimension 0
The draws below stay inside these ranges and needn't reach their ends.
There are 2 independent parts, one for each index of `slab`. The reference program is written for one: setup_inputs(seed, part) draws one part's arguments, and reference() takes and returns one part's arrays. A program takes and returns all parts, laid end to end along the dimension named above; an argument that names none is the same for every part. Nothing has to cross between parts.
All inputs are finite; a program needn't handle non-finite values. No bound on the sum of `incidence` on one device may be relied on, other than what follows from the above.
Results may differ from the reference program's by a relative error of at most 0.0062.
Values may be sent and summed in bfloat16 or wider, within the bound.
A program may use at most 128 MiB of HBM per device.

```python
import jax
import jax.numpy as jnp
from jax import lax

BINS = 2048
C = 32
W = 128
PT = 2048
TILES = 4
ANG = 64
Z = 16
NPIX = 8192


def touch_ends(values, own_key, low, high):
    index_at = [jax.random.randint(jax.random.fold_in(own_key, axis), (), 0, length) for axis, length in enumerate(values.shape)]
    longest = values.shape.index(max(values.shape))
    beside = index_at[:longest] + [(index_at[longest] + 1) % values.shape[longest]] + index_at[longest + 1:]
    return values.at[tuple(index_at)].set(low).at[tuple(beside)].set(high)


def block_levels(own_key, dims, cuts, smallest, top_value):
    level, own = 1.0, jax.random.fold_in(own_key, 6)
    for dim, shards_of in cuts:
        heights = jnp.exp(jax.random.uniform(jax.random.fold_in(own, dim), (shards_of,), jnp.float32, smallest / len(cuts), top_value / len(cuts)))
        level = level * jnp.repeat(heights, dims[dim] // shards_of).reshape([-1 if axis == dim else 1 for axis in range(len(dims))])
    return level


def noise(key, shape, deviation, most, shards=(), kind=jnp.bfloat16):
    values = jax.random.normal(key, shape, jnp.float32) * deviation
    if len(shards) > 0:
        values = block_levels(key, shape, shards, -0.22, 0.18) * values
    return jnp.clip(values, min=-most, max=most).astype(kind)


def setup_inputs(seed: int = 0, part: int = 0) -> dict:
    key_list = jax.random.split(jax.random.key(seed), 15)
    own_keys = jax.random.split(jax.random.fold_in(key_list[14], part), 15)
    primal = noise(own_keys[0], (Z, NPIX), 1.0, 6.0, ((0, 2), (1, 4)), jnp.float32)
    dual = noise(own_keys[1], (Z, ANG, BINS), 1.0, 6.0, ((0, 2), (1, 8)), jnp.float32)
    data = noise(own_keys[2], (Z, ANG, BINS), 1.0, 6.0, ((0, 2), (1, 8)), jnp.float32)
    blocks = noise(key_list[3], (TILES, ANG, PT, W), PT ** -0.5, 0.125, ((0, 4), (1, 2)))
    offsets = touch_ends(jax.random.randint(key_list[4], (TILES, ANG), 0, BINS - W + 1), jax.random.fold_in(key_list[4], 1), 0, BINS - W).astype(jnp.int32)
    incidence = touch_ends((jax.random.randint(key_list[5], (TILES, ANG), 0, 4) < 3).astype(jnp.int32), jax.random.fold_in(key_list[5], 1), 0, 1)
    dual_in = noise(key_list[6], (3, C), 0.7, 4.0, (), jnp.float32)
    dual_bias = noise(key_list[7], (C,), 0.5, 3.0, (), jnp.float32)
    dual_out = noise(key_list[8], (C,), C ** -0.5, 1.0, (), jnp.float32)
    kernel_in = noise(key_list[9], (3, 2, C), 6 ** -0.5, 2.5, (), jnp.float32)
    kernel_bias = noise(key_list[10], (C,), 0.5, 3.0, (), jnp.float32)
    kernel_out = noise(key_list[11], (3, C), (3 * C) ** -0.5, 0.625, (), jnp.float32)
    cot_primal = noise(own_keys[12], (Z, NPIX), 1.0, 6.0, ((0, 2), (1, 4)), jnp.float32)
    cot_dual = noise(own_keys[13], (Z, ANG, BINS), 1.0, 6.0, ((0, 2), (1, 8)), jnp.float32)
    return dict(primal=primal, dual=dual, data=data, blocks=blocks, offsets=offsets, incidence=incidence, dual_in=dual_in, dual_bias=dual_bias, dual_out=dual_out, kernel_in=kernel_in, kernel_bias=kernel_bias, kernel_out=kernel_out, cot_primal=cot_primal, cot_dual=cot_dual)


def place_windows(windows, starts):

    def place_one(window_rows, begin_at):
        blank = jnp.zeros((window_rows.shape[0], BINS), jnp.float32)
        return lax.dynamic_update_slice(blank, window_rows, (jnp.zeros((), jnp.int32), begin_at.astype(jnp.int32)))
    return jax.vmap(place_one, in_axes=(1, 0), out_axes=1)(windows, starts)

def take_windows(whole, starts):

    def take_one(row_block, begin_at):
        return lax.dynamic_slice(row_block, (jnp.zeros((), jnp.int32), begin_at.astype(jnp.int32)), (row_block.shape[0], W))
    return jax.vmap(take_one, in_axes=(1, 0), out_axes=1)(whole, starts)

def project_all(image_half, blocks, offsets, incidence):

    def step_tile(running, tile_at):
        tile_piece = lax.dynamic_slice_in_dim(image_half, tile_at * PT, PT, 1).astype(jnp.float32)
        block_set = blocks[tile_at].astype(jnp.float32)
        products = jnp.einsum('zp,apw->zaw', tile_piece, block_set, precision=lax.Precision.HIGHEST)
        products = products * incidence[tile_at].astype(jnp.float32)[None, :, None]
        return (running + place_windows(products, offsets[tile_at]), None)
    running, _ = lax.scan(step_tile, jnp.zeros((Z, ANG, BINS), jnp.float32), jnp.arange(TILES, dtype=jnp.int32))
    return running

def back_all(sino_half, blocks, offsets, incidence):

    def step_tile(unused, tile_at):
        windows = take_windows(sino_half, offsets[tile_at]).astype(jnp.float32)
        windows = windows * incidence[tile_at].astype(jnp.float32)[None, :, None]
        image_part = jnp.einsum('zaw,apw->zp', windows, blocks[tile_at].astype(jnp.float32), precision=lax.Precision.HIGHEST)
        return (unused, image_part)
    _, parts = lax.scan(step_tile, jnp.zeros((), jnp.float32), jnp.arange(TILES, dtype=jnp.int32))
    return jnp.transpose(parts, (1, 0, 2)).reshape(Z, TILES * PT)

def slope_of(values):
    return jax.jvp(jax.nn.gelu, (values,), (jnp.ones_like(values),))[1]

def widen(weights):
    return weights[:, None, None, None]

def dual_forward(dual, sinogram, data, dual_in, dual_bias, dual_out):
    pre_dual = widen(dual_in[0]) * dual[None] + widen(dual_in[1]) * sinogram[None] + widen(dual_in[2]) * data[None] + widen(dual_bias)
    new_dual = dual + lax.optimization_barrier(jnp.sum(widen(dual_out) * jax.nn.gelu(pre_dual), axis=0))
    return (pre_dual, new_dual)

def dual_backward(pre_dual, grad_new, dual_in, dual_out):
    grad_units = widen(dual_out) * slope_of(pre_dual) * grad_new[None]
    grad_dual = grad_new + lax.optimization_barrier(jnp.sum(widen(dual_in[0]) * grad_units, axis=0))
    grad_data = lax.optimization_barrier(jnp.sum(widen(dual_in[2]) * grad_units, axis=0))
    grad_sino = lax.optimization_barrier(jnp.sum(widen(dual_in[1]) * grad_units, axis=0))
    return (grad_dual, grad_data, grad_sino)

def conv_in(padded, kernel_in, kernel_bias):
    count = padded.shape[1] - 2
    pre_primal = jnp.broadcast_to(kernel_bias[:, None, None], (kernel_bias.shape[0], count, padded.shape[2]))
    for tap_index in range(3):
        pre_primal = pre_primal + jnp.einsum('ic,izp->czp', kernel_in[tap_index], padded[:, tap_index:tap_index + count], precision=lax.Precision.HIGHEST)
    return pre_primal

def hidden_grad(cot_padded, kernel_out):
    count = cot_padded.shape[1] - 2
    result = jnp.zeros((kernel_out.shape[1], count, cot_padded.shape[2]), jnp.float32)
    for tap_index in range(3):
        result = result + jnp.einsum('c,zp->czp', kernel_out[tap_index], cot_padded[0, 2 - tap_index:2 - tap_index + count], precision=lax.Precision.HIGHEST)
    return result

def input_grad(grad_padded, kernel_in):
    count = grad_padded.shape[1] - 2
    result = jnp.zeros((2, count, grad_padded.shape[2]), jnp.float32)
    for tap_index in range(3):
        result = result + jnp.einsum('ic,czp->izp', kernel_in[tap_index], grad_padded[:, 2 - tap_index:2 - tap_index + count], precision=lax.Precision.HIGHEST)
    return result

def pad_slices(values):
    return jnp.pad(values, ((0, 0), (1, 1), (0, 0)))

def reference(primal, dual, data, blocks, offsets, incidence, dual_in, dual_bias, dual_out, kernel_in, kernel_bias, kernel_out, cot_primal, cot_dual):
    image_half = lax.optimization_barrier(primal.astype(jnp.bfloat16))
    sinogram = project_all(image_half, blocks, offsets, incidence)
    pre_dual, new_dual = dual_forward(dual, sinogram, data, dual_in, dual_bias, dual_out)
    dual_half = lax.optimization_barrier(new_dual.astype(jnp.bfloat16))
    back_image = back_all(dual_half, blocks, offsets, incidence)
    pre_primal = conv_in(pad_slices(jnp.stack([primal, back_image])), kernel_in, kernel_bias)
    grad_pre = hidden_grad(pad_slices(cot_primal[None]), kernel_out) * slope_of(pre_primal)
    grad_in = input_grad(pad_slices(grad_pre), kernel_in)
    back_half = lax.optimization_barrier(grad_in[1].astype(jnp.bfloat16))
    grad_new = cot_dual + project_all(back_half, blocks, offsets, incidence)
    grad_dual, grad_data, grad_sino = dual_backward(pre_dual, grad_new, dual_in, dual_out)
    sino_half = lax.optimization_barrier(grad_sino.astype(jnp.bfloat16))
    grad_primal = cot_primal + grad_in[0] + back_all(sino_half, blocks, offsets, incidence)
    return (grad_primal, grad_dual, grad_data)
```

```python
import functools

import jax
import jax.numpy as jnp
from jax import lax
from jax.experimental import pallas as pl
from jax.experimental.pallas import tpu as pltpu
from jax.sharding import PartitionSpec as P

LANES = 128
K1 = 0.7978845608028654
K3 = K1 * 0.044715
F32 = jnp.float32
BF16 = jnp.bfloat16
MESH = pl.DeviceIdType.MESH


def kernel(
    tiles, groups, cores,
    primal, dual, data, blocks, offsets, incidence, dual_in, dual_bias, dual_out,
    kernel_in, kernel_bias, kernel_out, cot_primal, cot_dual,
    grad_primal, grad_dual, grad_data,
    held, psend, precv, dstage, dsend, drecv, slopes, sino, fresh, turn, turn2, dense_primal,
    dense_cot, dense_back, hsend, hpart, hedge, gsend, gpart,
    load_sem, psend_sem, precv_sem, dsend_sem, drecv_sem, edge_send, edge_recv,
    hsend_sem, hrecv_sem, hedge_send, hedge_recv, gsend_sem, grecv_sem,
):
    rows = primal.shape[0]
    own = dual.shape[1]
    nb = dual.shape[2] // LANES
    np_ = primal.shape[1] // LANES
    chans = dual_bias.shape[0]
    me = lax.axis_index("tile")
    gz = lax.axis_index("gz")
    ang = lax.axis_index("ang")

    def owner_at(i):
        return lax.rem(me + i, tiles)

    loads = []
    for i in range(tiles):
        o = owner_at(i + 1)
        copy = pltpu.make_async_copy(
            blocks.at[pl.ds(o * own, own)], held.at[pl.ds(o * own, own)], load_sem.at[i]
        )
        copy.start()
        loads.append(copy)

    barrier = pltpu.get_barrier_semaphore()
    for i in range(1, tiles):
        pl.semaphore_signal(barrier, inc=1, device_id={"tile": owner_at(i)}, device_id_type=MESH)
    for i in range(1, cores):
        pl.semaphore_signal(
            barrier, inc=1, device_id={"ang": lax.rem(ang + i, cores)}, device_id_type=MESH
        )
    for has, step in ((gz > 0, -1), (gz < groups - 1, 1)):
        @pl.when(has)
        def _():
            for core in range(cores):
                pl.semaphore_signal(
                    barrier, inc=1, device_id={"gz": gz + step, "ang": core}, device_id_type=MESH
                )
    sides = (gz > 0).astype(jnp.int32) + (gz < groups - 1).astype(jnp.int32)
    if groups == 2:
        sides = 1
    pl.semaphore_wait(barrier, tiles - 1 + cores - 1 + cores * sides)

    def to_dense(value, target, first):
        for b in range(np_):
            turn[b * rows : (b + 1) * rows, :] = value[:, b * LANES : (b + 1) * LANES]
        for z in range(rows):
            target[(first + z) * np_ : (first + z + 1) * np_, :] = turn[pl.ds(z, np_, stride=rows), :]

    to_dense(primal[...], dense_primal, 2)
    to_dense(cot_primal[...], dense_cot, 2)
    edge = 2 * np_
    low_in = pl.ds(0, edge)
    low_own = pl.ds(edge, edge)
    high_own = pl.ds(rows * np_, edge)
    high_in = pl.ds((rows + 2) * np_, edge)

    def edge_copies(step):
        src, dst, side = (low_own, high_in, 0) if step < 0 else (high_own, low_in, 1)
        return [
            pltpu.make_async_remote_copy(
                src_ref=ref.at[src], dst_ref=ref.at[dst],
                send_sem=edge_send.at[side, n], recv_sem=edge_recv.at[side, n],
                device_id={"gz": gz + step}, device_id_type=MESH,
            )
            for n, ref in enumerate((dense_primal, dense_cot))
        ]

    for has, step in ((gz > 0, -1), (gz < groups - 1, 1)):
        @pl.when(has)
        def _():
            for copy in edge_copies(step):
                copy.start()

        @pl.when(jnp.logical_not(has))
        def _():
            where = low_in if step < 0 else high_in
            for ref in (dense_primal, dense_cot, dense_back):
                ref[where, :] = jnp.zeros((edge, LANES), F32)

    lane = lax.broadcasted_iota(jnp.int32, (own, LANES), 1)
    sub = lax.broadcasted_iota(jnp.int32, (own, LANES), 0)

    def home_blocks():
        result = []
        for t in range(tiles):
            at = jnp.zeros((own, LANES), jnp.int32)
            for j in range(own):
                at = jnp.where(sub == j, offsets[t, me * own + j], at)
            result.append((at >> 7) + (lane < (at & (LANES - 1))).astype(jnp.int32))
        return result

    def pcopy(ph, i):
        return pltpu.make_async_remote_copy(
            src_ref=psend.at[ph, i], dst_ref=precv.at[ph, me],
            send_sem=psend_sem.at[ph, i], recv_sem=precv_sem.at[ph, me],
            device_id={"tile": owner_at(i)}, device_id_type=MESH,
        )

    def dcopy(ph, i):
        return pltpu.make_async_remote_copy(
            src_ref=dsend.at[ph, i], dst_ref=drecv.at[ph, me],
            send_sem=dsend_sem.at[ph, i], recv_sem=drecv_sem.at[ph, me],
            device_id={"tile": owner_at(i)}, device_id_type=MESH,
        )

    def await_recv(buffer, sem, ph, i):
        o = owner_at(i)
        pltpu.make_async_remote_copy(
            src_ref=buffer.at[ph, o], dst_ref=buffer.at[ph, o],
            send_sem=sem.at[ph, o], recv_sem=sem.at[ph, o],
            device_id={"tile": o}, device_id_type=MESH,
        ).wait_recv()

    def pair_of(a):
        return jnp.concatenate([held[a], held[a + 1]], axis=1)

    def project(image, ph):
        for i in list(range(1, tiles)) + [0]:
            o = owner_at(i)
            if ph == 0:
                loads[(i - 1) % tiles].wait()

            def step(j, carry):
                a = o * own + 2 * j
                both = jnp.dot(image, pair_of(a), preferred_element_type=F32)
                for h in range(2):
                    part = both[:, h * LANES : (h + 1) * LANES]
                    part = part * incidence[me, a + h].astype(F32)
                    part = pltpu.roll(part, offsets[me, a + h] & (LANES - 1), 1)
                    where = pl.ds((2 * j + h) * rows, rows)
                    if i == 0:
                        precv[ph, me, where, :] = part
                    else:
                        psend[ph, i, where, :] = part
                return carry

            lax.fori_loop(0, own // 2, step, 0)
            if i > 0:
                pcopy(ph, i).start()
        for i in range(1, tiles):
            await_recv(precv, precv_sem, ph, i)

    def place(ph, z, homes):
        windows = [precv.at[ph, t][pl.ds(z, own, stride=rows), :] for t in range(tiles)]
        result = []
        for b in range(nb):
            total = jnp.zeros((own, LANES), F32)
            for t in range(tiles):
                total = total + jnp.where(homes[t] == b, windows[t], 0.0)
            result.append(total)
        return result

    def take(values, z, homes):
        for t in range(tiles):
            total = jnp.zeros((own, LANES), F32)
            for b in range(nb):
                total = jnp.where(homes[t] == b, values[b], total)
            dstage.at[t][pl.ds(z, own, stride=rows), :] = total

    def send_windows(ph):
        for i in range(1, tiles):
            dsend[ph, i] = dstage[owner_at(i)].astype(BF16)
            dcopy(ph, i).start()
        drecv[ph, me] = dstage[me].astype(BF16)

    def back(ph):
        total = jnp.zeros((rows, np_ * LANES), F32)
        for i in range(tiles):
            o = owner_at(i)
            if i > 0:
                await_recv(drecv, drecv_sem, ph, i)

            def step(j, total):
                a = o * own + 2 * j
                both = drecv[ph, o, pl.ds(pl.multiple_of(2 * rows * j, 2 * rows), 2 * rows), :].astype(F32)
                parts = []
                for h in range(2):
                    part = both[h * rows : (h + 1) * rows] * incidence[me, a + h].astype(F32)
                    shift = (LANES - (offsets[me, a + h] & (LANES - 1))) & (LANES - 1)
                    parts.append(pltpu.roll(part, shift, 1))
                both = jnp.concatenate(parts, axis=1).astype(BF16)
                return total + lax.dot_general(
                    both, pair_of(a), (((1,), (1,)), ((), ())), preferred_element_type=F32
                )

            total = lax.fori_loop(0, own // 2, step, total)
        return total

    project(primal[...].astype(BF16), 0)
    group = 4
    unroll = 8

    def dual_row(z, carry):
        homes = home_blocks()
        for b, value in enumerate(place(0, z, homes)):
            sino[:, b * LANES : (b + 1) * LANES] = value

        def dual_piece(g, carry):
            cols = [
                pl.ds(pl.multiple_of((g * group + n) * LANES, LANES), LANES) for n in range(group)
            ]
            ds = [dual[z, :, col] for col in cols]
            ss = [sino[:, col] for col in cols]
            xs = [data[z, :, col] for col in cols]

            def channels(cu, sums):
                sums = [list(s) for s in sums]
                for k in range(unroll):
                    c = cu * unroll + k
                    w0, w1, w2 = dual_in[0, c], dual_in[1, c], dual_in[2, c]
                    bias, half = dual_bias[c], 0.5 * dual_out[c]
                    h0, h1, h2 = half * w0, half * w1, half * w2
                    for n in range(group):
                        x = w0 * ds[n] + w1 * ss[n] + w2 * xs[n] + bias
                        x2 = x * x
                        t = jnp.tanh(x * (K1 + K3 * x2))
                        up = 1.0 + t
                        slope = up * (1.0 + x * (1.0 - t) * (K1 + 3.0 * K3 * x2))
                        sums[0][n] = sums[0][n] + half * (x * up)
                        sums[1][n] = sums[1][n] + h0 * slope
                        sums[2][n] = sums[2][n] + h1 * slope
                        sums[3][n] = sums[3][n] + h2 * slope
                return tuple(tuple(s) for s in sums)

            zero = tuple(jnp.zeros((own, LANES), F32) for _ in range(group))
            sums = lax.fori_loop(0, chans // unroll, channels, (zero,) * 4)
            for n, col in enumerate(cols):
                fresh[:, col] = ds[n] + sums[0][n]
                for k in range(3):
                    slopes[k, z, :, col] = sums[k + 1][n]
            return carry

        lax.fori_loop(0, nb // group, dual_piece, 0)
        take([fresh[:, b * LANES : (b + 1) * LANES] for b in range(nb)], z, homes)
        return carry

    lax.fori_loop(0, rows, dual_row, 0)
    send_windows(0)

    to_dense(back(0), hsend, 0)

    def hcopy(i):
        return pltpu.make_async_remote_copy(
            src_ref=hsend, dst_ref=hpart.at[ang],
            send_sem=hsend_sem.at[i], recv_sem=hrecv_sem.at[ang],
            device_id={"ang": lax.rem(ang + i, cores)}, device_id_type=MESH,
        )

    def hedge_copies(step):
        src, side = (pl.ds(0, edge), 1) if step < 0 else (pl.ds((rows - 2) * np_, edge), 0)
        return [
            pltpu.make_async_remote_copy(
                src_ref=hsend.at[src], dst_ref=hedge.at[side, ang],
                send_sem=hedge_send.at[side, core], recv_sem=hedge_recv.at[side, ang],
                device_id={"gz": gz + step, "ang": core}, device_id_type=MESH,
            )
            for core in range(cores)
        ]

    for has, step in ((gz > 0, -1), (gz < groups - 1, 1)):
        @pl.when(has)
        def _():
            for copy in hedge_copies(step):
                copy.start()
    for i in range(1, cores):
        hcopy(i).start()
    hpart[ang] = hsend[...]

    for has, step in ((gz > 0, -1), (gz < groups - 1, 1)):
        @pl.when(has)
        def _():
            side = 1 if step < 0 else 0
            for copy in edge_copies(-step):
                copy.wait_recv()
            total = jnp.zeros((edge, LANES), F32)
            for core in range(cores):
                pltpu.make_async_remote_copy(
                    src_ref=hedge.at[1 - side, core], dst_ref=hedge.at[1 - side, core],
                    send_sem=hedge_recv.at[1 - side, core], recv_sem=hedge_recv.at[1 - side, core],
                    device_id={"gz": gz + step, "ang": core}, device_id_type=MESH,
                ).wait_recv()
                total = total + hedge[1 - side, core]
            dense_back[low_in if step < 0 else high_in, :] = total
    for i in range(1, cores):
        other = lax.rem(ang + i, cores)
        pltpu.make_async_remote_copy(
            src_ref=hpart.at[other], dst_ref=hpart.at[other],
            send_sem=hrecv_sem.at[other], recv_sem=hrecv_sem.at[other],
            device_id={"ang": other}, device_id_type=MESH,
        ).wait_recv()
    total = hpart[0]
    for core in range(1, cores):
        total = total + hpart[core]
    dense_back[pl.ds(edge, rows * np_), :] = total

    keep_low = (gz > 0).astype(F32)
    keep_high = (gz < groups - 1).astype(F32)

    def pixel_piece(h, carry):
        def at(ref, z):
            return ref[pl.ds(pl.multiple_of((z + 2) * np_ + h * 8, 8), 8), :]

        def channel(c, sums):
            sums = [list(s) for s in sums]
            kin = [[kernel_in[k, i, c] for i in range(2)] for k in range(3)]
            kout = [0.5 * kernel_out[k, c] for k in range(3)]
            bias = kernel_bias[c]
            for z in range(-1, rows + 1):
                x = bias + jnp.zeros((8, LANES), F32)
                hid = None
                for k in range(3):
                    x = x + kin[k][0] * at(dense_primal, z + k - 1)
                    x = x + kin[k][1] * at(dense_back, z + k - 1)
                    term = kout[k] * at(dense_cot, z - k + 1)
                    hid = term if hid is None else hid + term
                x2 = x * x
                t = jnp.tanh(x * (K1 + K3 * x2))
                grad = hid * ((1.0 + t) * (1.0 + x * (1.0 - t) * (K1 + 3.0 * K3 * x2)))
                if z < 0:
                    grad = grad * keep_low
                if z == rows:
                    grad = grad * keep_high
                for k in range(3):
                    out = z + k - 1
                    if 0 <= out < rows:
                        for i in range(2):
                            sums[i][out] = sums[i][out] + kin[k][i] * grad
            return tuple(tuple(s) for s in sums)

        zero = tuple(jnp.zeros((8, LANES), F32) for _ in range(rows))
        sums = lax.fori_loop(0, chans, channel, (zero,) * 2)
        for z in range(rows):
            turn[pl.ds(h * 8 * rows + z, 8, stride=rows), :] = sums[1][z]
            turn2[pl.ds(h * 8 * rows + z, 8, stride=rows), :] = sums[0][z]
        return carry

    lax.fori_loop(0, np_ // 8, pixel_piece, 0)
    image = jnp.concatenate([turn[b * rows : (b + 1) * rows, :] for b in range(np_)], axis=1)

    project(image.astype(BF16), 1)

    def grad_row(z, carry):
        homes = home_blocks()
        outs = []
        for b, value in enumerate(place(1, z, homes)):
            col = slice(b * LANES, (b + 1) * LANES)
            value = value + cot_dual[z, :, col]
            grad_dual[z, :, col] = value + value * slopes[0, z, :, col]
            grad_data[z, :, col] = value * slopes[2, z, :, col]
            outs.append(value * slopes[1, z, :, col])
        take(outs, z, homes)
        return carry

    lax.fori_loop(0, rows, grad_row, 0)
    send_windows(1)
    gsend[...] = back(1)

    def gcopy(i):
        return pltpu.make_async_remote_copy(
            src_ref=gsend, dst_ref=gpart.at[ang],
            send_sem=gsend_sem.at[i], recv_sem=grecv_sem.at[ang],
            device_id={"ang": lax.rem(ang + i, cores)}, device_id_type=MESH,
        )

    for i in range(1, cores):
        gcopy(i).start()
    gpart[ang] = gsend[...]
    for i in range(1, cores):
        other = lax.rem(ang + i, cores)
        pltpu.make_async_remote_copy(
            src_ref=gpart.at[other], dst_ref=gpart.at[other],
            send_sem=grecv_sem.at[other], recv_sem=grecv_sem.at[other],
            device_id={"ang": other}, device_id_type=MESH,
        ).wait_recv()
    total = gpart[0]
    for core in range(1, cores):
        total = total + gpart[core]
    for b in range(np_):
        col = slice(b * LANES, (b + 1) * LANES)
        grad_primal[:, col] = (
            cot_primal[:, col] + turn2[b * rows : (b + 1) * rows, :] + total[:, col]
        )

    for ph in range(2):
        for i in range(1, tiles):
            pcopy(ph, i).wait_send()
            dcopy(ph, i).wait_send()
    for i in range(1, cores):
        hcopy(i).wait_send()
        gcopy(i).wait_send()
    for has, step in ((gz > 0, -1), (gz < groups - 1, 1)):
        @pl.when(has)
        def _():
            for copy in edge_copies(step) + hedge_copies(step):
                copy.wait_send()


def solution(mesh):
    tiles, groups, cores = mesh.shape["tile"], mesh.shape["gz"], mesh.shape["ang"]

    def local(primal, dual, data, blocks, *rest):
        rows, pixels = primal.shape
        own, bins = dual.shape[1:]
        np_ = pixels // LANES
        dma = pltpu.SemaphoreType.DMA
        vmem = pl.BlockSpec(memory_space=pltpu.VMEM)
        smem = pl.BlockSpec(memory_space=pltpu.SMEM)
        window = (own * rows, LANES)
        scratch = [
            pltpu.VMEM(blocks.shape[1:], BF16),
            pltpu.VMEM((2, tiles) + window, F32),
            pltpu.VMEM((2, tiles) + window, F32),
            pltpu.VMEM((tiles,) + window, F32),
            pltpu.VMEM((2, tiles) + window, BF16),
            pltpu.VMEM((2, tiles) + window, BF16),
            pltpu.VMEM((3, rows, own, bins), F32),
            pltpu.VMEM((own, bins), F32),
            pltpu.VMEM((own, bins), F32),
            pltpu.VMEM((np_ * rows, LANES), F32),
            pltpu.VMEM((np_ * rows, LANES), F32),
            pltpu.VMEM(((rows + 4) * np_, LANES), F32),
            pltpu.VMEM(((rows + 4) * np_, LANES), F32),
            pltpu.VMEM(((rows + 4) * np_, LANES), F32),
            pltpu.VMEM((rows * np_, LANES), F32),
            pltpu.VMEM((cores, rows * np_, LANES), F32),
            pltpu.VMEM((2, cores, 2 * np_, LANES), F32),
            pltpu.VMEM((rows, pixels), F32),
            pltpu.VMEM((cores, rows, pixels), F32),
            dma((tiles,)),
            dma((2, tiles)), dma((2, tiles)), dma((2, tiles)), dma((2, tiles)),
            dma((2, 2)), dma((2, 2)),
            dma((cores,)), dma((cores,)), dma((2, cores)), dma((2, cores)),
            dma((cores,)), dma((cores,)),
        ]
        shape = jax.ShapeDtypeStruct
        return pl.pallas_call(
            functools.partial(kernel, tiles, groups, cores),
            out_shape=(
                shape((rows, pixels), F32),
                shape((rows, own, bins), F32),
                shape((rows, own, bins), F32),
            ),
            in_specs=[vmem, vmem, vmem, pl.BlockSpec(memory_space=pl.ANY)] + [smem] * 8 + [vmem] * 2,
            out_specs=(vmem, vmem, vmem),
            scratch_shapes=scratch,
            compiler_params=pltpu.CompilerParams(
                collective_id=0, has_side_effects=True, vmem_limit_bytes=48 * 2**20
            ),
        )(primal, dual, data, blocks[0], *rest)

    image = P(("slab", "gz"), "tile")
    sinogram = P(("slab", "gz"), ("ang", "tile"), None)
    angles = P(None, "ang")
    return jax.shard_map(
        local,
        mesh=mesh,
        in_specs=(
            image, sinogram, sinogram, P("tile", "ang", None, None), angles, angles,
            P(), P(), P(), P(), P(), P(), image, sinogram,
        ),
        out_specs=(image, sinogram, sinogram),
        check_vma=False,
    )
```

```python
import functools

import jax
import jax.numpy as jnp
from jax import lax
from jax.experimental import pallas as pl
from jax.experimental.pallas import tpu as pltpu
from jax.sharding import PartitionSpec as P

LANES = 128
K1 = 0.7978845608028654
K3 = K1 * 0.044715
SCALE = K3 ** (1.0 / 3.0)
KY = K1 / SCALE
F32 = jnp.float32
BF16 = jnp.bfloat16
MESH = pl.DeviceIdType.MESH


def kernel(
    tiles, groups, cores,
    primal_hbm, dual_hbm, data_hbm, blocks, offsets_hbm, incidence_hbm, dual_in_hbm, dual_bias_hbm,
    dual_out_hbm, kernel_in_hbm, kernel_bias_hbm, kernel_out_hbm, cot_primal_hbm, cot_dual_hbm,
    grad_primal, grad_dual, grad_data,
    primal, dual, data, offsets, incidence, dual_in, dual_bias,
    dual_out, kernel_in, kernel_bias, kernel_out, cot_primal, cot_dual, small_sem,
    base, pixel_base, pixel_hid, pstage,
    held, psend, precv, dstage, dsend, drecv, slopes, sino, fresh, turn, turn2, dense_primal,
    dense_cot, dense_back, hsend, hpart, hedge, gsend, gpart,
    load_sem, psend_sem, precv_sem, dsend_sem, drecv_sem, edge_send, edge_recv,
    hsend_sem, hrecv_sem, hedge_send, hedge_recv, gsend_sem, grecv_sem,
):
    rows = primal.shape[0]
    own = dual.shape[1]
    nb = dual.shape[2] // LANES
    np_ = primal.shape[1] // LANES
    chans = dual_bias.shape[0]
    me = lax.axis_index("tile")
    gz = lax.axis_index("gz")
    ang = lax.axis_index("ang")

    def owner_at(i):
        return lax.rem(me + i, tiles)

    small = []
    for n, (src, dst) in enumerate((
        (dual_in_hbm, dual_in), (dual_bias_hbm, dual_bias), (dual_hbm, dual), (data_hbm, data),
        (primal_hbm, primal), (cot_primal_hbm, cot_primal), (offsets_hbm, offsets),
        (incidence_hbm, incidence), (dual_out_hbm, dual_out), (kernel_in_hbm, kernel_in),
        (kernel_bias_hbm, kernel_bias), (kernel_out_hbm, kernel_out), (cot_dual_hbm, cot_dual),
    )):
        copy = pltpu.make_async_copy(src, dst, small_sem.at[n])
        copy.start()
        small.append(copy)
    loads = []
    for i in range(tiles):
        o = owner_at(i + 1)
        copy = pltpu.make_async_copy(
            blocks.at[pl.ds(o * own, own)], held.at[pl.ds(o * own, own)], load_sem.at[i]
        )
        copy.start()
        loads.append(copy)

    barrier = pltpu.get_barrier_semaphore()
    for i in range(1, tiles):
        pl.semaphore_signal(barrier, inc=1, device_id={"tile": owner_at(i)}, device_id_type=MESH)
    for i in range(1, cores):
        pl.semaphore_signal(
            barrier, inc=1, device_id={"ang": lax.rem(ang + i, cores)}, device_id_type=MESH
        )
    for has, step in ((gz > 0, -1), (gz < groups - 1, 1)):
        @pl.when(has)
        def _():
            for core in range(cores):
                pl.semaphore_signal(
                    barrier, inc=1, device_id={"gz": gz + step, "ang": core}, device_id_type=MESH
                )
    sides = (gz > 0).astype(jnp.int32) + (gz < groups - 1).astype(jnp.int32)
    if groups == 2:
        sides = 1
    pl.semaphore_wait(barrier, tiles - 1 + cores - 1 + cores * sides)

    def to_dense(value, target, first):
        for b in range(np_):
            turn[b * rows : (b + 1) * rows, :] = value[:, b * LANES : (b + 1) * LANES]
        for z in range(rows):
            target[(first + z) * np_ : (first + z + 1) * np_, :] = turn[pl.ds(z, np_, stride=rows), :]

    for copy in small:
        copy.wait()
    to_dense(primal[...], dense_primal, 2)
    to_dense(cot_primal[...], dense_cot, 2)
    edge = 2 * np_
    low_in = pl.ds(0, edge)
    low_own = pl.ds(edge, edge)
    high_own = pl.ds(rows * np_, edge)
    high_in = pl.ds((rows + 2) * np_, edge)

    def edge_copies(step):
        src, dst, side = (low_own, high_in, 0) if step < 0 else (high_own, low_in, 1)
        return [
            pltpu.make_async_remote_copy(
                src_ref=ref.at[src], dst_ref=ref.at[dst],
                send_sem=edge_send.at[side, n], recv_sem=edge_recv.at[side, n],
                device_id={"gz": gz + step}, device_id_type=MESH,
            )
            for n, ref in enumerate((dense_primal, dense_cot))
        ]

    for has, step in ((gz > 0, -1), (gz < groups - 1, 1)):
        @pl.when(has)
        def _():
            for copy in edge_copies(step):
                copy.start()

        @pl.when(jnp.logical_not(has))
        def _():
            where = low_in if step < 0 else high_in
            for ref in (dense_primal, dense_cot, dense_back):
                ref[where, :] = jnp.zeros((edge, LANES), F32)

    lane = lax.broadcasted_iota(jnp.int32, (own, LANES), 1)
    sub = lax.broadcasted_iota(jnp.int32, (own, LANES), 0)

    def home_blocks():
        result = []
        for i in range(tiles):
            at = jnp.zeros((own, LANES), jnp.int32)
            for j in range(own):
                at = jnp.where(sub == j, offsets[owner_at(i), me * own + j], at)
            result.append((at >> 7) + (lane < (at & (LANES - 1))).astype(jnp.int32))
        return result

    def pcopy(ph, i):
        return pltpu.make_async_remote_copy(
            src_ref=psend.at[ph, i], dst_ref=precv.at[ph, me],
            send_sem=psend_sem.at[ph, i], recv_sem=precv_sem.at[ph, me],
            device_id={"tile": owner_at(i)}, device_id_type=MESH,
        )

    def dcopy(ph, i):
        return pltpu.make_async_remote_copy(
            src_ref=dsend.at[ph, i], dst_ref=drecv.at[ph, me],
            send_sem=dsend_sem.at[ph, i], recv_sem=drecv_sem.at[ph, me],
            device_id={"tile": owner_at(i)}, device_id_type=MESH,
        )

    def await_recv(buffer, sem, ph, i):
        o = owner_at(i)
        pltpu.make_async_remote_copy(
            src_ref=buffer.at[ph, o], dst_ref=buffer.at[ph, o],
            send_sem=sem.at[ph, o], recv_sem=sem.at[ph, o],
            device_id={"tile": o}, device_id_type=MESH,
        ).wait_recv()

    def pair_of(a):
        return jnp.concatenate([held[a], held[a + 1]], axis=1)

    def project(image, ph):
        for i in list(range(1, tiles)) + [0]:
            o = owner_at(i)
            if ph == 0:
                loads[(i - 1) % tiles].wait()

            def step(j, carry):
                a = o * own + 2 * j
                both = jnp.dot(image, pair_of(a), preferred_element_type=F32)
                for h in range(2):
                    part = both[:, h * LANES : (h + 1) * LANES]
                    part = part * incidence[me, a + h].astype(F32)
                    part = pltpu.roll(part, offsets[me, a + h] & (LANES - 1), 1)
                    where = pl.ds((2 * j + h) * rows, rows)
                    pstage[i, where, :] = part
                return carry

            lax.fori_loop(0, own // 2, step, 0)
            if i > 0:
                psend[ph, i] = pstage[i].astype(BF16)
                pcopy(ph, i).start()

    def projected(ph):
        for i in range(1, tiles):
            await_recv(precv, precv_sem, ph, i)
            pstage[i] = precv[ph, owner_at(i)].astype(F32)

    def place(z):
        windows = [pstage.at[i][pl.ds(z, own, stride=rows), :] for i in range(tiles)]
        result = []
        for b in range(nb):
            total = jnp.zeros((own, LANES), F32)
            for t in range(tiles):
                total = total + jnp.where(homes[t] == b, windows[t], 0.0)
            result.append(total)
        return result

    def take(values, z):
        for t in range(tiles):
            total = jnp.zeros((own, LANES), F32)
            for b in range(nb):
                total = jnp.where(homes[t] == b, values[b], total)
            dstage.at[t][pl.ds(z, own, stride=rows), :] = total

    def send_windows(ph):
        for i in range(1, tiles):
            dsend[ph, i] = dstage[i].astype(BF16)
            dcopy(ph, i).start()
        drecv[ph, me] = dstage[0].astype(BF16)

    def back(ph):
        total = jnp.zeros((rows, np_ * LANES), F32)
        for i in range(tiles):
            o = owner_at(i)
            if i > 0:
                await_recv(drecv, drecv_sem, ph, i)

            def step(j, total):
                a = o * own + 2 * j
                both = drecv[ph, o, pl.ds(pl.multiple_of(2 * rows * j, 2 * rows), 2 * rows), :].astype(F32)
                parts = []
                for h in range(2):
                    part = both[h * rows : (h + 1) * rows] * incidence[me, a + h].astype(F32)
                    shift = (LANES - (offsets[me, a + h] & (LANES - 1))) & (LANES - 1)
                    parts.append(pltpu.roll(part, shift, 1))
                both = jnp.concatenate(parts, axis=1).astype(BF16)
                return total + lax.dot_general(
                    both, pair_of(a), (((1,), (1,)), ((), ())), preferred_element_type=F32
                )

            total = lax.fori_loop(0, own // 2, step, total)
        return total

    homes = home_blocks()

    def base_piece(at, carry):
        zz, b = at // nb, at % nb
        col = pl.ds(pl.multiple_of(b * LANES, LANES), LANES)
        d = jnp.concatenate([dual[2 * zz, :, col], dual[2 * zz + 1, :, col]], axis=0)
        x = jnp.concatenate([data[2 * zz, :, col], data[2 * zz + 1, :, col]], axis=0)
        for c in range(chans):
            base[zz, b, c] = (
                (SCALE * dual_in[0, c]) * d + (SCALE * dual_in[2, c]) * x + SCALE * dual_bias[c]
            )
        return carry

    lax.fori_loop(0, rows // 2 * nb, base_piece, 0)

    project(primal[...].astype(BF16), 0)
    for has, step in ((gz > 0, -1), (gz < groups - 1, 1)):
        @pl.when(has)
        def _():
            for copy in edge_copies(-step):
                copy.wait_recv()

    def dense_at(ref, z, h):
        return ref[pl.ds(pl.multiple_of((z + 2) * np_ + h * 8, 8), 8), :]

    def pixel_first(at, carry):
        h, c = at // chans, at % chans
        for z in range(-1, rows + 1):
            x = jnp.full((8, LANES), SCALE * kernel_bias[c], F32)
            hid = jnp.zeros((8, LANES), F32)
            for k in range(3):
                x = x + (SCALE * kernel_in[k, 0, c]) * dense_at(dense_primal, z + k - 1, h)
                hid = hid + (1.5 * kernel_out[k, c]) * dense_at(dense_cot, z - k + 1, h)
            pixel_base[h, c, z + 1] = x
            pixel_hid[h, c, z + 1] = hid
        return carry

    lax.fori_loop(0, np_ // 8 * chans, pixel_first, 0)
    projected(0)
    group = 2
    unroll = 8

    def dual_row(zz, carry):
        for n in range(2):
            for b, value in enumerate(place(2 * zz + n)):
                sino[n * own : (n + 1) * own, b * LANES : (b + 1) * LANES] = value

        def dual_piece(g, carry):
            cols = [
                pl.ds(pl.multiple_of((g * group + n) * LANES, LANES), LANES) for n in range(group)
            ]
            ss = [sino[:, col] for col in cols]

            def channels(cu, sums):
                sums = [list(s) for s in sums]
                for k in range(unroll):
                    c = cu * unroll + k
                    w1 = SCALE * dual_in[1, c]
                    out = dual_out[c]
                    half = (0.5 / SCALE) * out
                    h0, h1, h2 = [1.5 * out * dual_in[m, c] for m in range(3)]
                    for n in range(group):
                        y = base[zz, g * group + n, c] + w1 * ss[n]
                        y2 = y * y
                        t = jnp.tanh(y * (KY + y2))
                        up = 1.0 + t
                        slope = up * (1.0 / 3.0 + (1.0 - t) * (y * (KY / 3.0 + y2)))
                        sums[0][n] = sums[0][n] + half * (y * up)
                        sums[1][n] = sums[1][n] + h0 * slope
                        sums[2][n] = sums[2][n] + h1 * slope
                        sums[3][n] = sums[3][n] + h2 * slope
                return tuple(tuple(s) for s in sums)

            zero = tuple(jnp.zeros((2 * own, LANES), F32) for _ in range(group))
            sums = lax.fori_loop(0, chans // unroll, channels, (zero,) * 4)
            for n, col in enumerate(cols):
                for m in range(2):
                    half_rows = slice(m * own, (m + 1) * own)
                    fresh[half_rows, col] = dual[2 * zz + m, :, col] + sums[0][n][half_rows]
                    for k in range(3):
                        slopes[k, 2 * zz + m, :, col] = sums[k + 1][n][half_rows]
            return carry

        lax.fori_loop(0, nb // group, dual_piece, 0)
        for n in range(2):
            half_rows = slice(n * own, (n + 1) * own)
            take([fresh[half_rows, b * LANES : (b + 1) * LANES] for b in range(nb)], 2 * zz + n)
        return carry

    lax.fori_loop(0, rows // 2, dual_row, 0)
    send_windows(0)

    to_dense(back(0), hsend, 0)

    def hcopy(i):
        return pltpu.make_async_remote_copy(
            src_ref=hsend, dst_ref=hpart.at[ang],
            send_sem=hsend_sem.at[i], recv_sem=hrecv_sem.at[ang],
            device_id={"ang": lax.rem(ang + i, cores)}, device_id_type=MESH,
        )

    def hedge_copies(step):
        src, side = (pl.ds(0, edge), 1) if step < 0 else (pl.ds((rows - 2) * np_, edge), 0)
        return [
            pltpu.make_async_remote_copy(
                src_ref=hsend.at[src], dst_ref=hedge.at[side, ang],
                send_sem=hedge_send.at[side, core], recv_sem=hedge_recv.at[side, ang],
                device_id={"gz": gz + step, "ang": core}, device_id_type=MESH,
            )
            for core in range(cores)
        ]

    for has, step in ((gz > 0, -1), (gz < groups - 1, 1)):
        @pl.when(has)
        def _():
            for copy in hedge_copies(step):
                copy.start()
    for i in range(1, cores):
        hcopy(i).start()
    hpart[ang] = hsend[...]

    for has, step in ((gz > 0, -1), (gz < groups - 1, 1)):
        @pl.when(has)
        def _():
            side = 1 if step < 0 else 0
            total = jnp.zeros((edge, LANES), F32)
            for core in range(cores):
                pltpu.make_async_remote_copy(
                    src_ref=hedge.at[1 - side, core], dst_ref=hedge.at[1 - side, core],
                    send_sem=hedge_recv.at[1 - side, core], recv_sem=hedge_recv.at[1 - side, core],
                    device_id={"gz": gz + step, "ang": core}, device_id_type=MESH,
                ).wait_recv()
                total = total + hedge[1 - side, core]
            dense_back[low_in if step < 0 else high_in, :] = total
    for i in range(1, cores):
        other = lax.rem(ang + i, cores)
        pltpu.make_async_remote_copy(
            src_ref=hpart.at[other], dst_ref=hpart.at[other],
            send_sem=hrecv_sem.at[other], recv_sem=hrecv_sem.at[other],
            device_id={"ang": other}, device_id_type=MESH,
        ).wait_recv()
    total = hpart[0]
    for core in range(1, cores):
        total = total + hpart[core]
    dense_back[pl.ds(edge, rows * np_), :] = total

    keep_low = (gz > 0).astype(F32)
    keep_high = (gz < groups - 1).astype(F32)

    def pixel_piece(h, carry):
        def channel(c, sums):
            sums = [list(s) for s in sums]
            kin = [[kernel_in[k, i, c] for i in range(2)] for k in range(3)]
            for z in range(-1, rows + 1):
                y = pixel_base[h, c, z + 1]
                for k in range(3):
                    y = y + (SCALE * kin[k][1]) * dense_at(dense_back, z + k - 1, h)
                y2 = y * y
                t = jnp.tanh(y * (KY + y2))
                slope = (1.0 + t) * (1.0 / 3.0 + (1.0 - t) * (y * (KY / 3.0 + y2)))
                grad = pixel_hid[h, c, z + 1] * slope
                if z < 0:
                    grad = grad * keep_low
                if z == rows:
                    grad = grad * keep_high
                for k in range(3):
                    out = z + k - 1
                    if 0 <= out < rows:
                        for i in range(2):
                            sums[i][out] = sums[i][out] + kin[k][i] * grad
            return tuple(tuple(s) for s in sums)

        zero = tuple(jnp.zeros((8, LANES), F32) for _ in range(rows))
        sums = lax.fori_loop(0, chans, channel, (zero,) * 2)
        for z in range(rows):
            turn[pl.ds(h * 8 * rows + z, 8, stride=rows), :] = sums[1][z]
            turn2[pl.ds(h * 8 * rows + z, 8, stride=rows), :] = sums[0][z]
        return carry

    lax.fori_loop(0, np_ // 8, pixel_piece, 0)
    image = jnp.concatenate([turn[b * rows : (b + 1) * rows, :] for b in range(np_)], axis=1)

    project(image.astype(BF16), 1)

    projected(1)

    def grad_row(z, carry):
        outs = []
        for b, value in enumerate(place(z)):
            col = slice(b * LANES, (b + 1) * LANES)
            value = value + cot_dual[z, :, col]
            grad_dual[z, :, col] = value + value * slopes[0, z, :, col]
            grad_data[z, :, col] = value * slopes[2, z, :, col]
            outs.append(value * slopes[1, z, :, col])
        take(outs, z)
        return carry

    lax.fori_loop(0, rows, grad_row, 0)
    send_windows(1)
    gsend[...] = back(1)

    def gcopy(i):
        return pltpu.make_async_remote_copy(
            src_ref=gsend, dst_ref=gpart.at[ang],
            send_sem=gsend_sem.at[i], recv_sem=grecv_sem.at[ang],
            device_id={"ang": lax.rem(ang + i, cores)}, device_id_type=MESH,
        )

    for i in range(1, cores):
        gcopy(i).start()
    gpart[ang] = gsend[...]
    for i in range(1, cores):
        other = lax.rem(ang + i, cores)
        pltpu.make_async_remote_copy(
            src_ref=gpart.at[other], dst_ref=gpart.at[other],
            send_sem=grecv_sem.at[other], recv_sem=grecv_sem.at[other],
            device_id={"ang": other}, device_id_type=MESH,
        ).wait_recv()
    total = gpart[0]
    for core in range(1, cores):
        total = total + gpart[core]
    for b in range(np_):
        col = slice(b * LANES, (b + 1) * LANES)
        grad_primal[:, col] = (
            cot_primal[:, col] + turn2[b * rows : (b + 1) * rows, :] + total[:, col]
        )

    for ph in range(2):
        for i in range(1, tiles):
            pcopy(ph, i).wait_send()
            dcopy(ph, i).wait_send()
    for i in range(1, cores):
        hcopy(i).wait_send()
        gcopy(i).wait_send()
    for has, step in ((gz > 0, -1), (gz < groups - 1, 1)):
        @pl.when(has)
        def _():
            for copy in edge_copies(step) + hedge_copies(step):
                copy.wait_send()


def solution(mesh):
    tiles, groups, cores = mesh.shape["tile"], mesh.shape["gz"], mesh.shape["ang"]

    def local(primal, dual, data, blocks, *rest):
        rows, pixels = primal.shape
        own, bins = dual.shape[1:]
        np_ = pixels // LANES
        dma = pltpu.SemaphoreType.DMA
        vmem = pl.BlockSpec(memory_space=pltpu.VMEM)
        window = (own * rows, LANES)
        args = (primal, dual, data) + rest
        smalls = [
            pltpu.SMEM(x.shape, x.dtype) if 2 < n < 11 else pltpu.VMEM(x.shape, x.dtype)
            for n, x in enumerate(args)
        ]
        chans = rest[3].shape[0]
        scratch = smalls + [
            dma((len(args),)),
            pltpu.VMEM((rows // 2, bins // LANES, chans, 2 * own, LANES), F32),
            pltpu.VMEM((np_ // 8, chans, rows + 2, 8, LANES), F32),
            pltpu.VMEM((np_ // 8, chans, rows + 2, 8, LANES), F32),
            pltpu.VMEM((tiles,) + window, F32),
            pltpu.VMEM(blocks.shape[1:], BF16),
            pltpu.VMEM((2, tiles) + window, BF16),
            pltpu.VMEM((2, tiles) + window, BF16),
            pltpu.VMEM((tiles,) + window, F32),
            pltpu.VMEM((2, tiles) + window, BF16),
            pltpu.VMEM((2, tiles) + window, BF16),
            pltpu.VMEM((3, rows, own, bins), F32),
            pltpu.VMEM((2 * own, bins), F32),
            pltpu.VMEM((2 * own, bins), F32),
            pltpu.VMEM((np_ * rows, LANES), F32),
            pltpu.VMEM((np_ * rows, LANES), F32),
            pltpu.VMEM(((rows + 4) * np_, LANES), F32),
            pltpu.VMEM(((rows + 4) * np_, LANES), F32),
            pltpu.VMEM(((rows + 4) * np_, LANES), F32),
            pltpu.VMEM((rows * np_, LANES), F32),
            pltpu.VMEM((cores, rows * np_, LANES), F32),
            pltpu.VMEM((2, cores, 2 * np_, LANES), F32),
            pltpu.VMEM((rows, pixels), F32),
            pltpu.VMEM((cores, rows, pixels), F32),
            dma((tiles,)),
            dma((2, tiles)), dma((2, tiles)), dma((2, tiles)), dma((2, tiles)),
            dma((2, 2)), dma((2, 2)),
            dma((cores,)), dma((cores,)), dma((2, cores)), dma((2, cores)),
            dma((cores,)), dma((cores,)),
        ]
        shape = jax.ShapeDtypeStruct
        return pl.pallas_call(
            functools.partial(kernel, tiles, groups, cores),
            out_shape=(
                shape((rows, pixels), F32),
                shape((rows, own, bins), F32),
                shape((rows, own, bins), F32),
            ),
            in_specs=[pl.BlockSpec(memory_space=pl.ANY)] * 14,
            out_specs=(vmem, vmem, vmem),
            scratch_shapes=scratch,
            compiler_params=pltpu.CompilerParams(
                collective_id=0, has_side_effects=True, vmem_limit_bytes=60 * 2**20
            ),
        )(primal, dual, data, blocks[0], *rest)

    image = P(("slab", "gz"), "tile")
    sinogram = P(("slab", "gz"), ("ang", "tile"), None)
    angles = P(None, "ang")
    return jax.shard_map(
        local,
        mesh=mesh,
        in_specs=(
            image, sinogram, sinogram, P("tile", "ang", None, None), angles, angles,
            P(), P(), P(), P(), P(), P(), image, sinogram,
        ),
        out_specs=(image, sinogram, sinogram),
        check_vma=False,
    )
```
